32 devices in a mesh: group: 2 (over y), expert: 16 (over z, x, core), tensor: 1.
Axes of the slice: x: 2, y: 2, z: 4, core: 2. Of those that a mesh axis runs over, the one named last changes fastest.
Arguments:
- tokens: bfloat16 [4096, 2048], P(('group', 'expert'), 'tensor'), parts along dimension 0, may hold values from -6 to 6
- expert_ids: int32 [4096, 8], P(('group', 'expert')), parts along dimension 0, may hold values from 0 to 15, all different within a row; in each aligned block of 128 rows (0 to 127, 128 to 255, ...) at most 128 rows name the same one
- gate_numer: int32 [4096, 8], P(('group', 'expert')), parts along dimension 0, may hold values from 1 to 255
- capacity: int32 [16], replicated, may hold values from 512 to 1535
- up_weight: bfloat16 [16, 2048, 768], P('expert', None, 'tensor'), may hold values from -0.125 to 0.125
- down_weight: bfloat16 [16, 768, 2048], P('expert', None, 'tensor'), may hold values from -0.21875 to 0.21875
Outputs:
- mixed: bfloat16 [4096, 2048], P(('group', 'expert'), 'tensor'), parts along dimension 0
The draws below stay inside these ranges and needn't reach their ends.
There are 2 independent parts, one for each index of `group`. The reference program is written for one: setup_inputs(seed, part) draws one part's arguments, and reference() takes and returns one part's arrays. A program takes and returns all parts, laid end to end along the dimension named above; an argument that names none is the same for every part. Nothing has to cross between parts.
Inputs may be any that keep to these rules, and one draw needn't show every extreme that they name: `expert_ids`: each token names 8 different experts. In each aligned block of 128 rows (the tokens of one index of expert) no expert is named more than 128 times, a bound that some block reaches.
All inputs are finite; a program needn't handle non-finite values.
Results may differ from the reference program's by a relative error of at most 0.0075.
Values may be sent and summed in bfloat16 or wider, within the bound.
A program may use at most 128 MiB of HBM per device.

```python
import math
import jax
import jax.numpy as jnp
import numpy as np
from jax import lax

D = 2048
H = 768
TOPK = 8
TOK_DEV = 128
EXPERTS = 16
TOKENS = 2048
CAP_SRC = 128
N_EXPERT = 16


def with_ends(values, rng, low, top_value):
    spot = [jax.random.randint(jax.random.fold_in(rng, axis), (), 0, length) for axis, length in enumerate(values.shape)]
    widest = values.shape.index(max(values.shape))
    next_to = spot[:widest] + [(spot[widest] + 1) % values.shape[widest]] + spot[widest + 1:]
    return values.at[tuple(spot)].set(low).at[tuple(next_to)].set(top_value)


def block_scale(own_key, extent, pieces, low, top_value):
    def one(position, parts):
        steps = jax.random.uniform(jax.random.fold_in(jax.random.fold_in(own_key, 6), position), (parts,), jnp.float32, low / len(pieces), top_value / len(pieces))
        return jnp.repeat(jnp.exp(steps), extent[position] // parts).reshape((-1,) + (1,) * (len(extent) - position - 1))

    loudness = one(*pieces[0])
    for cut in pieces[1:]:
        loudness = loudness * one(*cut)
    return loudness


def shared_out(rng, own, number, rows, number_of, top, reach, skew):
    ranking = jax.random.permutation(rng, number_of)
    crowded, common = shares(number_of, rows * top, reach, skew, True), shares(number_of, rows * top, reach, skew, False)
    places = jnp.arange(number_of)

    def named(sizes, rotation):
        used = int((sizes > 0).sum())
        fixed = max(1, used // 4)
        moved = fixed + (places - fixed + rotation * (used - fixed)) % max(1, number_of - fixed)
        return jnp.zeros((number_of,), jnp.int32).at[ranking[jnp.where(places < fixed, places, moved)]].set(jnp.asarray(sizes, jnp.int32))

    sizes = jnp.where(number % 4 == 0, named(crowded, number // 4), named(common, number - number // 4 - 1))
    mixed = jax.random.permutation(jax.random.fold_in(own, 3), number_of)
    giver, taker = mixed[0:number_of // 2 * 2:2], mixed[1:number_of // 2 * 2:2]
    slack = jnp.minimum(sizes[giver] - 1, reach - sizes[taker]) // 2
    slack = jnp.where((giver == ranking[0]) | (taker == ranking[0]) | (sizes[taker] == 0), 0, jnp.maximum(slack, 0))
    moved = jax.random.randint(jax.random.fold_in(own, 4), (number_of // 2,), 0, 1 << 20) % (slack + 1)
    sizes = sizes.at[giver].add(-moved).at[taker].add(moved)
    items = jnp.searchsorted(jnp.cumsum(sizes), jnp.arange(rows * top), side="right").astype(jnp.int32)
    grid = items.reshape(top, rows).T
    grid = grid[jax.random.permutation(jax.random.fold_in(own, 1), rows)]
    rotation = jax.random.randint(jax.random.fold_in(own, 2), (rows, 1), 0, top)
    return jnp.take_along_axis(grid, (jnp.arange(top)[None, :] + rotation) % top, axis=1)


def shares(count, total, limit, slope, full):
    portions = [(1 << 20) // math.isqrt(standing ** slope) + 1 for standing in range(1, count + 1)]
    largest = limit if full else min(limit, max(-(-total // count), total * portions[0] // sum(portions)))
    least = 1 if total - largest >= count - 1 else 0
    given, surplus = [largest] + [least] * (count - 1), total - largest - least * (count - 1)
    while surplus > 0:
        movable = [i for i in range(1, count) if given[i] < largest] or [i for i in range(1, count) if given[i] < limit]
        pool, left = sum([portions[i] for i in movable]), surplus
        for i in movable:
            addition = min(limit - given[i], max(1, left * portions[i] // pool), surplus)
            given[i] = given[i] + addition
            surplus = surplus - addition
    return np.array(given)


def noise(key, dims, scale, limit, split=(), held_as=jnp.bfloat16):
    entries = jax.random.normal(key, dims, jnp.float32) * scale
    if len(split) > 0:
        entries = block_scale(key, dims, split, -0.22, 0.18) * entries
    return jnp.clip(entries, min=-limit, max=limit).astype(held_as)


def setup_inputs(seed: int = 0, part: int = 0) -> dict:
    key_list = jax.random.split(jax.random.key(seed), 7)
    own_keys = jax.random.split(jax.random.fold_in(key_list[6], part), 7)
    tokens = noise(own_keys[0], (TOKENS, D), 1.0, 6.0, ((0, 16),))
    expert_ids_keys = jax.random.split(jax.random.fold_in(own_keys[1], 1), TOKENS // TOK_DEV)
    expert_ids_turns = jax.random.permutation(jax.random.fold_in(own_keys[1], 3), TOKENS // TOK_DEV)
    expert_ids = jax.vmap(lambda own, number: shared_out(jax.random.fold_in(own_keys[1], 2), own, number, TOK_DEV, EXPERTS, TOPK, CAP_SRC, 2))(expert_ids_keys, expert_ids_turns).reshape((TOKENS, TOPK))
    gate_numer = with_ends(jax.random.randint(own_keys[2], (TOKENS, TOPK), 1, 256), jax.random.fold_in(own_keys[2], 1), 1, 255).astype(jnp.int32)
    capacity = with_ends(jax.random.randint(key_list[3], (EXPERTS,), 4 * TOK_DEV, 12 * TOK_DEV), jax.random.fold_in(key_list[3], 1), 4 * TOK_DEV, (12 * TOK_DEV) - 1).astype(jnp.int32)
    up_weight = noise(key_list[4], (EXPERTS, D, H), D ** -0.5, 0.125, ((0, 16),))
    down_weight = noise(key_list[5], (EXPERTS, H, D), H ** -0.5, 0.21875, ((0, 16),))
    return dict(tokens=tokens, expert_ids=expert_ids, gate_numer=gate_numer, capacity=capacity, up_weight=up_weight, down_weight=down_weight)


def reference(tokens, expert_ids, gate_numer, capacity, up_weight, down_weight):
    total_rows, model_width = tokens.shape
    per_token = expert_ids.shape[1]
    experts = capacity.shape[0]
    slot_count = N_EXPERT * CAP_SRC
    chosen = expert_ids.reshape(-1)
    one_hot = (chosen[:, None] == jnp.arange(experts, dtype=jnp.int32)[None, :]).astype(jnp.int32)
    before = jnp.cumsum(one_hot, axis=0) - one_hot
    slot_rank = jnp.sum(before * one_hot, axis=1).astype(jnp.int32)
    retained = slot_rank < capacity[chosen]
    numerator = gate_numer.astype(jnp.float32)
    weighting = (numerator / jnp.sum(numerator, axis=1, keepdims=True)).reshape(-1)
    weighting = jnp.where(retained, weighting, jnp.zeros_like(weighting))
    token_of = (jnp.arange(total_rows * per_token, dtype=jnp.int32) // per_token).astype(jnp.int32)
    slot_token = jnp.full((experts, slot_count), total_rows, jnp.int32).at[chosen, slot_rank].set(token_of)
    slot_weight = jnp.zeros((experts, slot_count), jnp.float32).at[chosen, slot_rank].set(weighting)
    padded = jnp.concatenate([tokens, jnp.zeros((1, model_width), tokens.dtype)], axis=0)

    def one_expert(totals, packed):
        w_up, w_down, row_index, row_weight = packed
        inputs = padded[row_index]
        hidden = jax.nn.silu(jnp.dot(inputs, w_up, preferred_element_type=jnp.float32)).astype(jnp.bfloat16)
        result = jnp.dot(hidden, w_down, preferred_element_type=jnp.float32).astype(jnp.bfloat16)
        totals = totals.at[row_index].add(row_weight[:, None] * result.astype(jnp.float32), mode="drop")
        return totals, None

    totals, _ = lax.scan(one_expert, jnp.zeros((total_rows, model_width), jnp.float32),
                         (up_weight, down_weight, slot_token, slot_weight))
    return totals.astype(jnp.bfloat16)
```

```python
import jax
import jax.numpy as jnp
from jax import lax
from jax.sharding import PartitionSpec as P


def entering(part, axis, combine, identity):
    place = lax.axis_index(axis)
    gathered = lax.all_gather(part, axis)
    state = jnp.zeros_like(part) + jnp.asarray(identity, part.dtype)

    def one(lap, state):
        return combine(state, lax.dynamic_index_in_dim(gathered, lap, 0, False))

    return lax.fori_loop(0, place, one, state)


def add_counts(earlier, later):
    return earlier + later


def expert_work(received, up_matrix, down_matrix):
    sources, slot_count, half_width = received.shape
    hidden_half = up_matrix.shape[1]
    fragment = lax.all_gather(received, "tensor", axis=2, tiled=True)
    columns = fragment.shape[2]
    weights_block = up_matrix
    up_total = jnp.dot(
        fragment.reshape(-1, columns), weights_block, preferred_element_type=jnp.float32
    )
    hidden = jax.nn.silu(up_total).astype(jnp.bfloat16).reshape(sources, slot_count, hidden_half)
    fragment = lax.all_gather(hidden, "tensor", axis=2, tiled=True)
    columns = fragment.shape[2]
    weights_block = down_matrix
    down_total = jnp.dot(
        fragment.reshape(-1, columns), weights_block, preferred_element_type=jnp.float32
    )
    return down_total.astype(jnp.bfloat16).reshape(sources, slot_count, half_width)


def general(tokens, expert_ids, gate_numer, capacity, up_weight, down_weight):
    token_rows, half_width = tokens.shape
    per_token = expert_ids.shape[1]
    experts = capacity.shape[0]
    per_source = min(token_rows, 2 * token_rows * per_token // experts)
    chosen = expert_ids.reshape(-1)
    one_hot = (chosen[:, None] == jnp.arange(experts, dtype=jnp.int32)[None, :]).astype(jnp.int32)
    counts = jnp.sum(one_hot, axis=0)
    local_rank = jnp.sum((jnp.cumsum(one_hot, axis=0) - one_hot) * one_hot, axis=1)
    prefix = entering(counts, "expert", add_counts, jnp.zeros_like(counts))
    global_rank = local_rank + jnp.sum(one_hot * prefix[None, :], axis=1)
    limit = jnp.sum(one_hot * capacity[None, :], axis=1)
    retained = global_rank < limit
    numerator = gate_numer.astype(jnp.float32)
    weighting = (numerator / jnp.sum(numerator, axis=1, keepdims=True)).reshape(-1)
    weighting = jnp.where(retained, weighting, jnp.zeros_like(weighting))
    token_of = jnp.arange(token_rows * per_token, dtype=jnp.int32) // per_token
    slot_table = (
        jnp.full((experts, per_source), token_rows, jnp.int32).at[chosen, local_rank].set(token_of)
    )
    source = jnp.concatenate([tokens, jnp.zeros((1, half_width), tokens.dtype)], axis=0)
    up_matrix = up_weight[0]
    down_matrix = down_weight[0]
    outgoing = source[slot_table]
    arrived = lax.all_to_all(outgoing, "expert", split_axis=0, concat_axis=0, tiled=True)
    returned = lax.all_to_all(
        expert_work(arrived, up_matrix, down_matrix),
        "expert",
        split_axis=0,
        concat_axis=0,
        tiled=True,
    )
    picked = returned[chosen, local_rank]
    weighted = picked.astype(jnp.float32) * weighting[:, None]
    mixed = jnp.sum(weighted.reshape(token_rows, per_token, picked.shape[1]), axis=1)
    return mixed.astype(jnp.bfloat16)


def column_weight(chosen, numer, capacity, expert):
    hit = chosen == expert
    named = jnp.any(hit, axis=1)
    rank = jnp.cumsum(named.astype(jnp.int32)) - named.astype(jnp.int32)
    gate = jnp.sum(jnp.where(hit, numer, 0), axis=1).astype(jnp.float32)
    weight = gate / jnp.sum(numer, axis=1).astype(jnp.float32)
    return jnp.where(rank < capacity[expert], weight, 0.0)


def dense(tokens, expert_ids, gate_numer, capacity, up_weight, down_weight):
    per_token = expert_ids.shape[1]
    place = lax.axis_index("expert")
    routing = lax.all_gather(
        jnp.concatenate([expert_ids, gate_numer], axis=1), "expert", tiled=True
    )
    rows = lax.all_gather(tokens, "expert", tiled=True)
    weight = column_weight(routing[:, :per_token], routing[:, per_token:], capacity, place)
    hidden = jnp.dot(rows, up_weight[0], preferred_element_type=jnp.float32)
    hidden = jax.nn.silu(hidden).astype(jnp.bfloat16)
    result = jnp.dot(hidden, down_weight[0], preferred_element_type=jnp.float32)
    part = (weight[:, None] * result).astype(jnp.bfloat16)
    return lax.psum_scatter(part, "expert", scatter_dimension=0, tiled=True)


def solution(mesh):
    one_each = mesh.shape["tensor"] == 1 and mesh.shape["expert"] <= 16
    local = dense if one_each else general
    in_specs = (
        P(("group", "expert"), "tensor"),
        P(("group", "expert"), None),
        P(("group", "expert"), None),
        P(),
        P("expert", None, "tensor"),
        P("expert", None, "tensor"),
    )
    out_specs = P(("group", "expert"), "tensor")
    return jax.shard_map(local, mesh=mesh, in_specs=in_specs, out_specs=out_specs, check_vma=False)
```

```python
import functools

import jax
import jax.numpy as jnp
from jax import lax
from jax.experimental import pallas as pl
from jax.experimental.pallas import tpu as pltpu
from jax.sharding import PartitionSpec as P


def entering(part, axis, combine, identity):
    place = lax.axis_index(axis)
    gathered = lax.all_gather(part, axis)
    state = jnp.zeros_like(part) + jnp.asarray(identity, part.dtype)

    def one(lap, state):
        return combine(state, lax.dynamic_index_in_dim(gathered, lap, 0, False))

    return lax.fori_loop(0, place, one, state)


def add_counts(earlier, later):
    return earlier + later


def expert_work(received, up_matrix, down_matrix):
    sources, slot_count, half_width = received.shape
    hidden_half = up_matrix.shape[1]
    fragment = lax.all_gather(received, "tensor", axis=2, tiled=True)
    columns = fragment.shape[2]
    weights_block = up_matrix
    up_total = jnp.dot(
        fragment.reshape(-1, columns), weights_block, preferred_element_type=jnp.float32
    )
    hidden = jax.nn.silu(up_total).astype(jnp.bfloat16).reshape(sources, slot_count, hidden_half)
    fragment = lax.all_gather(hidden, "tensor", axis=2, tiled=True)
    columns = fragment.shape[2]
    weights_block = down_matrix
    down_total = jnp.dot(
        fragment.reshape(-1, columns), weights_block, preferred_element_type=jnp.float32
    )
    return down_total.astype(jnp.bfloat16).reshape(sources, slot_count, half_width)


def general(tokens, expert_ids, gate_numer, capacity, up_weight, down_weight):
    token_rows, half_width = tokens.shape
    per_token = expert_ids.shape[1]
    experts = capacity.shape[0]
    per_source = min(token_rows, 2 * token_rows * per_token // experts)
    chosen = expert_ids.reshape(-1)
    one_hot = (chosen[:, None] == jnp.arange(experts, dtype=jnp.int32)[None, :]).astype(jnp.int32)
    counts = jnp.sum(one_hot, axis=0)
    local_rank = jnp.sum((jnp.cumsum(one_hot, axis=0) - one_hot) * one_hot, axis=1)
    prefix = entering(counts, "expert", add_counts, jnp.zeros_like(counts))
    global_rank = local_rank + jnp.sum(one_hot * prefix[None, :], axis=1)
    limit = jnp.sum(one_hot * capacity[None, :], axis=1)
    retained = global_rank < limit
    numerator = gate_numer.astype(jnp.float32)
    weighting = (numerator / jnp.sum(numerator, axis=1, keepdims=True)).reshape(-1)
    weighting = jnp.where(retained, weighting, jnp.zeros_like(weighting))
    token_of = jnp.arange(token_rows * per_token, dtype=jnp.int32) // per_token
    slot_table = (
        jnp.full((experts, per_source), token_rows, jnp.int32).at[chosen, local_rank].set(token_of)
    )
    source = jnp.concatenate([tokens, jnp.zeros((1, half_width), tokens.dtype)], axis=0)
    up_matrix = up_weight[0]
    down_matrix = down_weight[0]
    outgoing = source[slot_table]
    arrived = lax.all_to_all(outgoing, "expert", split_axis=0, concat_axis=0, tiled=True)
    returned = lax.all_to_all(
        expert_work(arrived, up_matrix, down_matrix),
        "expert",
        split_axis=0,
        concat_axis=0,
        tiled=True,
    )
    picked = returned[chosen, local_rank]
    weighted = picked.astype(jnp.float32) * weighting[:, None]
    mixed = jnp.sum(weighted.reshape(token_rows, per_token, picked.shape[1]), axis=1)
    return mixed.astype(jnp.bfloat16)


def add_rows(dst, *parts):
    @pl.loop(0, dst.shape[0] // 16)
    def _(i):
        rows = pl.ds(pl.multiple_of(i * 16, 16), 16)
        total = parts[0][rows, :].astype(jnp.float32)
        for part in parts[1:]:
            total = total + part[rows, :].astype(jnp.float32)
        dst[rows, :] = total.astype(dst.dtype)


def routed_weights(meta, capacity, weights, place, nz):
    slots, _, block = meta.shape
    half = meta.shape[1] // 2
    c, x, z = place % 2, (place // 2) % 2, place // 4

    def block_of(r):
        cf, xf, k = r // (2 * nz), (r // nz) % 2, r % nz
        zs = z - k
        zs = jnp.where(zs < 0, zs + nz, zs)
        return zs * 4 + (x + xf - 2 * x * xf) * 2 + (c + cf - 2 * c * cf)

    ids = meta[:, :half, :].astype(jnp.float32)
    gates = meta[:, half:, :].astype(jnp.float32)
    hit = (ids == place.astype(jnp.float32)).astype(jnp.float32)
    named = jnp.sum(hit, axis=1)
    gate = jnp.sum(hit * gates, axis=1)
    whole = jnp.sum(gates, axis=1)
    row = lax.broadcasted_iota(jnp.int32, (block, block), 0)
    col = lax.broadcasted_iota(jnp.int32, (block, block), 1)
    earlier = (row < col).astype(jnp.bfloat16)
    inside = jnp.dot(named.astype(jnp.bfloat16), earlier, preferred_element_type=jnp.float32)
    later_slot = lax.broadcasted_iota(jnp.int32, (slots, slots), 0)
    early_slot = lax.broadcasted_iota(jnp.int32, (slots, slots), 1)
    lower = (block_of(early_slot) < block_of(later_slot)).astype(jnp.bfloat16)
    before = jnp.dot(lower, named.astype(jnp.bfloat16), preferred_element_type=jnp.float32)
    rank = inside + jnp.sum(before, axis=1, keepdims=True)
    limit = capacity[place].astype(jnp.float32)
    spread = jnp.where(rank < limit, gate / whole, 0.0)
    weights[...] = jnp.zeros_like(weights)
    weights[0:slots, :] = spread
    weights[...] = weights[...].T


def block_work(rows, hidden, up, down, weights, slot, keep, give):
    width = 256
    block = keep.shape[0]

    @pl.loop(0, up.shape[1] // width)
    def _(i):
        cols = pl.ds(pl.multiple_of(i * width, width), width)
        v = jnp.dot(rows[...].reshape(2 * block, rows.shape[-1]), up[:, cols], preferred_element_type=jnp.float32)
        hidden[:, cols] = (v / (1.0 + jnp.exp(-v))).astype(jnp.bfloat16)

    mine = weights[:, slot[0] : slot[0] + 1]
    other = weights[:, slot[1] : slot[1] + 1]

    @pl.loop(0, down.shape[1] // width)
    def _(i):
        cols = pl.ds(pl.multiple_of(i * width, width), width)
        v = jnp.dot(hidden[...], down[:, cols], preferred_element_type=jnp.float32)
        keep[:, cols] = (v[:block] * mine).astype(jnp.bfloat16)
        give[:, cols] = (v[block:] * other).astype(jnp.bfloat16)


def kernel(
    nz, tokens_hbm, meta_in, capacity, up_hbm, down_hbm, out,
    held, meta, up, down, hidden, weights, keep, give, from_core, from_x, from_z,
    local_sem, meta_send, meta_recv, gz_send, gx_send, gc_send, g_recv,
    rc_send, rc_recv, rx_send, rx_recv, rz_send, rz_recv,
):
    place = lax.axis_index("expert")
    c, x, z = place % 2, (place // 2) % 2, place // 4
    sibling = place + 1 - 2 * c
    across = place + 2 - 4 * x
    block = tokens_hbm.shape[0]

    def along(k):
        return lax.rem(place + 4 * k, 4 * nz)

    def remote(src, dst, send, recv, target):
        copy = pltpu.make_async_remote_copy(
            src_ref=src, dst_ref=dst, send_sem=send, recv_sem=recv,
            device_id={"expert": target}, device_id_type=pl.DeviceIdType.MESH,
        )
        copy.start()
        sent.append(copy)

    def arrived(ref, sem):
        pltpu.make_async_copy(ref, ref, sem).wait()

    sent = []
    loads = [
        pltpu.make_async_copy(tokens_hbm, held.at[0, 0, 0], local_sem.at[0]),
        pltpu.make_async_copy(up_hbm.at[0], up, local_sem.at[1]),
        pltpu.make_async_copy(down_hbm.at[0], down, local_sem.at[2]),
    ]
    for load in loads:
        load.start()
    meta[0] = meta_in[...]

    barrier = pltpu.get_barrier_semaphore()
    partners = [sibling, across] + [along(k) for k in range(1, nz)]
    for partner in partners:
        pl.semaphore_signal(
            barrier, inc=1, device_id={"expert": partner}, device_id_type=pl.DeviceIdType.MESH
        )
    pl.semaphore_wait(barrier, len(partners))

    def gather_across(k):
        remote(held.at[k, 0, 0], held.at[k, 1, 0], gx_send.at[k], g_recv.at[k, 1, 0], across)

    def gather_core(k, xf):
        remote(held.at[k, xf, 0], held.at[k, xf, 1], gc_send.at[k, xf], g_recv.at[k, xf, 1], sibling)

    def gathered(k, xf, cf):
        arrived(held.at[k, xf, cf], g_recv.at[k, xf, cf])

    for k in range(1, nz):
        remote(meta.at[0], meta.at[k], meta_send.at[k], meta_recv.at[k], along(k))
    loads[0].wait()
    for k in range(1, nz):
        remote(held.at[0, 0, 0], held.at[k, 0, 0], gz_send.at[k], g_recv.at[k, 0, 0], along(k))
    gather_core(0, 0)
    for k in range(1, nz):
        arrived(meta.at[k], meta_recv.at[k])
    remote(meta.at[0:nz], meta.at[nz : 2 * nz], meta_send.at[0], meta_recv.at[0], across)
    gather_across(0)
    arrived(meta.at[nz : 2 * nz], meta_recv.at[0])
    remote(meta.at[0 : 2 * nz], meta.at[2 * nz : 4 * nz], meta_send.at[nz], meta_recv.at[nz], sibling)
    arrived(meta.at[2 * nz : 4 * nz], meta_recv.at[nz])
    routed_weights(meta, capacity, weights, place, nz)
    loads[1].wait()
    loads[2].wait()

    def work(k, xf):
        gathered(k, xf, 1)
        rows = held.at[k, xf]
        slot = (xf * nz + k, (2 + xf) * nz + k)
        block_work(rows, hidden, up, down, weights, slot, keep.at[k, xf], give.at[k, xf])
        remote(give.at[k, xf], from_core.at[k, xf], rc_send.at[k, xf], rc_recv.at[k, xf], sibling)

    def sum_for_across(k):
        arrived(from_core.at[k, 1], rc_recv.at[k, 1])
        add_rows(keep.at[k, 1], keep.at[k, 1], from_core.at[k, 1])
        remote(keep.at[k, 1], from_x.at[k], rx_send.at[k], rx_recv.at[k], across)

    def sum_for_along(k):
        arrived(from_core.at[k, 0], rc_recv.at[k, 0])
        arrived(from_x.at[k], rx_recv.at[k])
        add_rows(keep.at[k, 0], keep.at[k, 0], from_core.at[k, 0], from_x.at[k])
        remote(keep.at[k, 0], from_z.at[k], rz_send.at[k], rz_recv.at[k], along(nz - k))

    work(0, 0)
    for k in range(1, nz):
        gathered(k, 0, 0)
        gather_across(k)
        gather_core(k, 0)
        gathered(k - 1, 1, 0)
        gather_core(k - 1, 1)
        work(k - 1, 1)
        work(k, 0)
        sum_for_across(k - 1)
        if k >= 3:
            sum_for_along(k - 2)
    gathered(nz - 1, 1, 0)
    gather_core(nz - 1, 1)
    work(nz - 1, 1)
    if nz >= 3:
        sum_for_along(nz - 2)
    sum_for_across(nz - 1)
    if nz >= 2:
        sum_for_along(nz - 1)
    arrived(from_core.at[0, 0], rc_recv.at[0, 0])
    arrived(from_x.at[0], rx_recv.at[0])
    for k in range(1, nz):
        arrived(from_z.at[k], rz_recv.at[k])
    add_rows(out, keep.at[0, 0], from_core.at[0, 0], from_x.at[0], *[from_z.at[k] for k in range(1, nz)])
    for copy in sent:
        copy.wait_send()


def fused(size, tokens, expert_ids, gate_numer, capacity, up_weight, down_weight):
    nz = size // 4
    block, columns = tokens.shape
    inner = up_weight.shape[2]
    routing = jnp.concatenate([expert_ids, gate_numer], axis=1).astype(jnp.bfloat16).T
    anywhere = pl.BlockSpec(memory_space=pl.ANY)
    near = pl.BlockSpec(memory_space=pltpu.VMEM)
    wide = jnp.bfloat16
    dma = pltpu.SemaphoreType.DMA
    return pl.pallas_call(
        functools.partial(kernel, nz),
        out_shape=jax.ShapeDtypeStruct((block, columns), tokens.dtype),
        in_specs=[anywhere, near, pl.BlockSpec(memory_space=pltpu.SMEM), anywhere, anywhere],
        out_specs=near,
        scratch_shapes=[
            pltpu.VMEM((nz, 2, 2, block, columns), wide),
            pltpu.VMEM((size,) + routing.shape, wide),
            pltpu.VMEM((columns, inner), wide),
            pltpu.VMEM((inner, columns), wide),
            pltpu.VMEM((2 * block, inner), wide),
            pltpu.VMEM((block, block), jnp.float32),
            pltpu.VMEM((nz, 2, block, columns), wide),
            pltpu.VMEM((nz, 2, block, columns), wide),
            pltpu.VMEM((nz, 2, block, columns), wide),
            pltpu.VMEM((nz, block, columns), wide),
            pltpu.VMEM((nz, block, columns), wide),
            dma((3,)), dma((nz + 1,)), dma((nz + 1,)),
            dma((nz,)), dma((nz,)), dma((nz, 2)), dma((nz, 2, 2)),
            dma((nz, 2)), dma((nz, 2)), dma((nz,)), dma((nz,)), dma((nz,)), dma((nz,)),
        ],
        compiler_params=pltpu.CompilerParams(
            collective_id=0, has_side_effects=True, vmem_limit_bytes=56 * 2**20
        ),
        cost_estimate=pl.CostEstimate(
            flops=4 * size * block * columns * inner, bytes_accessed=4 * columns * inner, transcendentals=0
        ),
    )(tokens, routing, capacity, up_weight, down_weight)


def solution(mesh):
    size = mesh.shape["expert"]
    fits = mesh.shape["tensor"] == 1 and size % 4 == 0 and size <= 16
    local = functools.partial(fused, size) if fits else general
    in_specs = (
        P(("group", "expert"), "tensor"),
        P(("group", "expert"), None),
        P(("group", "expert"), None),
        P(),
        P("expert", None, "tensor"),
        P("expert", None, "tensor"),
    )
    out_specs = P(("group", "expert"), "tensor")
    return jax.shard_map(local, mesh=mesh, in_specs=in_specs, out_specs=out_specs, check_vma=False)
```

```python
import functools

import jax
import jax.numpy as jnp
from jax import lax
from jax.experimental import pallas as pl
from jax.experimental.pallas import tpu as pltpu
from jax.sharding import PartitionSpec as P


def entering(part, axis, combine, identity):
    place = lax.axis_index(axis)
    gathered = lax.all_gather(part, axis)
    state = jnp.zeros_like(part) + jnp.asarray(identity, part.dtype)

    def one(lap, state):
        return combine(state, lax.dynamic_index_in_dim(gathered, lap, 0, False))

    return lax.fori_loop(0, place, one, state)


def add_counts(earlier, later):
    return earlier + later


def expert_work(received, up_matrix, down_matrix):
    sources, slot_count, half_width = received.shape
    hidden_half = up_matrix.shape[1]
    fragment = lax.all_gather(received, "tensor", axis=2, tiled=True)
    columns = fragment.shape[2]
    weights_block = up_matrix
    up_total = jnp.dot(
        fragment.reshape(-1, columns), weights_block, preferred_element_type=jnp.float32
    )
    hidden = jax.nn.silu(up_total).astype(jnp.bfloat16).reshape(sources, slot_count, hidden_half)
    fragment = lax.all_gather(hidden, "tensor", axis=2, tiled=True)
    columns = fragment.shape[2]
    weights_block = down_matrix
    down_total = jnp.dot(
        fragment.reshape(-1, columns), weights_block, preferred_element_type=jnp.float32
    )
    return down_total.astype(jnp.bfloat16).reshape(sources, slot_count, half_width)


def general(tokens, expert_ids, gate_numer, capacity, up_weight, down_weight):
    token_rows, half_width = tokens.shape
    per_token = expert_ids.shape[1]
    experts = capacity.shape[0]
    per_source = min(token_rows, 2 * token_rows * per_token // experts)
    chosen = expert_ids.reshape(-1)
    one_hot = (chosen[:, None] == jnp.arange(experts, dtype=jnp.int32)[None, :]).astype(jnp.int32)
    counts = jnp.sum(one_hot, axis=0)
    local_rank = jnp.sum((jnp.cumsum(one_hot, axis=0) - one_hot) * one_hot, axis=1)
    prefix = entering(counts, "expert", add_counts, jnp.zeros_like(counts))
    global_rank = local_rank + jnp.sum(one_hot * prefix[None, :], axis=1)
    limit = jnp.sum(one_hot * capacity[None, :], axis=1)
    retained = global_rank < limit
    numerator = gate_numer.astype(jnp.float32)
    weighting = (numerator / jnp.sum(numerator, axis=1, keepdims=True)).reshape(-1)
    weighting = jnp.where(retained, weighting, jnp.zeros_like(weighting))
    token_of = jnp.arange(token_rows * per_token, dtype=jnp.int32) // per_token
    slot_table = (
        jnp.full((experts, per_source), token_rows, jnp.int32).at[chosen, local_rank].set(token_of)
    )
    source = jnp.concatenate([tokens, jnp.zeros((1, half_width), tokens.dtype)], axis=0)
    up_matrix = up_weight[0]
    down_matrix = down_weight[0]
    outgoing = source[slot_table]
    arrived = lax.all_to_all(outgoing, "expert", split_axis=0, concat_axis=0, tiled=True)
    returned = lax.all_to_all(
        expert_work(arrived, up_matrix, down_matrix),
        "expert",
        split_axis=0,
        concat_axis=0,
        tiled=True,
    )
    picked = returned[chosen, local_rank]
    weighted = picked.astype(jnp.float32) * weighting[:, None]
    mixed = jnp.sum(weighted.reshape(token_rows, per_token, picked.shape[1]), axis=1)
    return mixed.astype(jnp.bfloat16)


def add_rows(dst, *parts):
    @pl.loop(0, dst.shape[0] // 16)
    def _(i):
        rows = pl.ds(pl.multiple_of(i * 16, 16), 16)
        total = parts[0][rows, :].astype(jnp.float32)
        for part in parts[1:]:
            total = total + part[rows, :].astype(jnp.float32)
        dst[rows, :] = total.astype(dst.dtype)


def nearest(at, nz):
    offsets = [0]
    for distance in range(1, nz):
        for source in (at - distance, at + distance):
            if 0 <= source < nz:
                offsets.append((at - source) % nz)
    return offsets


def routed_weights(meta, capacity, weights, place, nz):
    slots, _, block = meta.shape
    half = meta.shape[1] // 2
    c, x, z = place % 2, (place // 2) % 2, place // 4

    def block_of(r):
        cf, xf, k = r // (2 * nz), (r // nz) % 2, r % nz
        zs = z - k
        zs = jnp.where(zs < 0, zs + nz, zs)
        return zs * 4 + (x + xf - 2 * x * xf) * 2 + (c + cf - 2 * c * cf)

    ids = meta[:, :half, :].astype(jnp.float32)
    gates = meta[:, half:, :].astype(jnp.float32)
    hit = (ids == place.astype(jnp.float32)).astype(jnp.float32)
    named = jnp.sum(hit, axis=1)
    gate = jnp.sum(hit * gates, axis=1)
    whole = jnp.sum(gates, axis=1)
    row = lax.broadcasted_iota(jnp.int32, (block, block), 0)
    col = lax.broadcasted_iota(jnp.int32, (block, block), 1)
    earlier = (row < col).astype(jnp.bfloat16)
    inside = jnp.dot(named.astype(jnp.bfloat16), earlier, preferred_element_type=jnp.float32)
    later_slot = lax.broadcasted_iota(jnp.int32, (slots, slots), 0)
    early_slot = lax.broadcasted_iota(jnp.int32, (slots, slots), 1)
    lower = (block_of(early_slot) < block_of(later_slot)).astype(jnp.bfloat16)
    before = jnp.dot(lower, named.astype(jnp.bfloat16), preferred_element_type=jnp.float32)
    rank = inside + jnp.sum(before, axis=1, keepdims=True)
    limit = capacity[place].astype(jnp.float32)
    spread = jnp.where(rank < limit, gate / whole, 0.0)
    weights[...] = jnp.zeros_like(weights)
    weights[0:slots, :] = spread
    weights[...] = weights[...].T


def block_work(rows, hidden, up, down, weights, slot, keep, give):
    width = 256
    block = keep.shape[0]

    @pl.loop(0, up.shape[1] // width)
    def _(i):
        cols = pl.ds(pl.multiple_of(i * width, width), width)
        v = jnp.dot(rows[...].reshape(2 * block, rows.shape[-1]), up[:, cols], preferred_element_type=jnp.float32)
        hidden[:, cols] = (v / (1.0 + jnp.exp(-v))).astype(jnp.bfloat16)

    lane = lax.broadcasted_iota(jnp.int32, weights.shape, 1)
    mine = jnp.sum(jnp.where(lane == slot[0], weights[...], 0.0), axis=1, keepdims=True)
    other = jnp.sum(jnp.where(lane == slot[1], weights[...], 0.0), axis=1, keepdims=True)

    @pl.loop(0, down.shape[1] // width)
    def _(i):
        cols = pl.ds(pl.multiple_of(i * width, width), width)
        v = jnp.dot(hidden[...], down[:, cols], preferred_element_type=jnp.float32)
        keep[:, cols] = (v[:block] * mine).astype(jnp.bfloat16)
        give[:, cols] = (v[block:] * other).astype(jnp.bfloat16)


def kernel(
    nz, tokens_hbm, meta_in, capacity, up_hbm, down_hbm, out,
    held, meta, up, down, hidden, weights, keep, give, from_core, from_x, from_z,
    local_sem, meta_send, meta_recv, gz_send, gx_send, gc_send, g_recv,
    rc_send, rc_recv, rx_send, rx_recv, rz_send, rz_recv,
):
    place = lax.axis_index("expert")
    c, x, z = place % 2, (place // 2) % 2, place // 4
    sibling = place + 1 - 2 * c
    across = place + 2 - 4 * x
    block = tokens_hbm.shape[0]

    def along(k):
        return lax.rem(place + 4 * k, 4 * nz)

    def remote(src, dst, send, recv, target, when=None):
        copy = pltpu.make_async_remote_copy(
            src_ref=src, dst_ref=dst, send_sem=send, recv_sem=recv,
            device_id={"expert": target}, device_id_type=pl.DeviceIdType.MESH,
        )
        if when is None:
            copy.start()
        else:
            pl.when(when)(copy.start)
        sent.append((copy, when))

    def arrived(ref, sem):
        pltpu.make_async_copy(ref, ref, sem).wait()

    sent = []
    loads = [
        pltpu.make_async_copy(tokens_hbm, held.at[0, 0, 0], local_sem.at[0]),
        pltpu.make_async_copy(up_hbm.at[0], up, local_sem.at[1]),
        pltpu.make_async_copy(down_hbm.at[0], down, local_sem.at[2]),
    ]
    for load in loads:
        load.start()
    meta[0] = meta_in[...]

    barrier = pltpu.get_barrier_semaphore()
    partners = [sibling, across] + [along(k) for k in range(1, nz)]
    for partner in partners:
        pl.semaphore_signal(
            barrier, inc=1, device_id={"expert": partner}, device_id_type=pl.DeviceIdType.MESH
        )
    pl.semaphore_wait(barrier, len(partners))

    steps = [
        functools.reduce(lambda a, s: a + s, [jnp.where(z == at, nearest(at, nz)[i], 0) for at in range(nz)])
        for i in range(nz)
    ]

    def gather_along(i):
        k = steps[i]
        rising = k <= z
        step = jnp.where(rising, 1, -1)
        target = jnp.clip(z + step, 0, nz - 1)
        slot = jnp.clip(k + step, 0, nz - 1)
        remote(
            held.at[k, 0, 0], held.at[slot, 0, 0], gz_send.at[i], g_recv.at[slot, 0, 0],
            place + 4 * (target - z), target != z,
        )

    def gather_own():
        up_z, down_z = jnp.minimum(z + 1, nz - 1), jnp.maximum(z - 1, 0)
        remote(
            held.at[0, 0, 0], held.at[1 % nz, 0, 0], gz_send.at[0], g_recv.at[1 % nz, 0, 0],
            place + 4 * (up_z - z), up_z != z,
        )
        remote(
            held.at[0, 0, 0], held.at[nz - 1, 0, 0], gz_send.at[nz], g_recv.at[nz - 1, 0, 0],
            place + 4 * (down_z - z), down_z != z,
        )

    def gather_across(i):
        k = steps[i]
        remote(held.at[k, 0, 0], held.at[k, 1, 0], gx_send.at[i], g_recv.at[k, 1, 0], across)

    def gather_core(i, xf):
        k = steps[i]
        remote(held.at[k, xf, 0], held.at[k, xf, 1], gc_send.at[i, xf], g_recv.at[k, xf, 1], sibling)

    def gathered(i, xf, cf):
        k = steps[i]
        arrived(held.at[k, xf, cf], g_recv.at[k, xf, cf])

    for k in range(1, nz):
        remote(meta.at[0], meta.at[k], meta_send.at[k], meta_recv.at[k], along(k))
    loads[0].wait()
    gather_own()
    gather_core(0, 0)
    for k in range(1, nz):
        arrived(meta.at[k], meta_recv.at[k])
    remote(meta.at[0:nz], meta.at[nz : 2 * nz], meta_send.at[0], meta_recv.at[0], across)
    gather_across(0)
    arrived(meta.at[nz : 2 * nz], meta_recv.at[0])
    remote(meta.at[0 : 2 * nz], meta.at[2 * nz : 4 * nz], meta_send.at[nz], meta_recv.at[nz], sibling)
    arrived(meta.at[2 * nz : 4 * nz], meta_recv.at[nz])
    routed_weights(meta, capacity, weights, place, nz)
    loads[1].wait()
    loads[2].wait()

    def work(i, xf):
        gathered(i, xf, 1)
        k = steps[i]
        slot = (xf * nz + k, (2 + xf) * nz + k)
        block_work(held.at[k, xf], hidden, up, down, weights, slot, keep.at[i, xf], give.at[i, xf])
        remote(give.at[i, xf], from_core.at[i, xf], rc_send.at[i, xf], rc_recv.at[i, xf], sibling)

    def sum_for_across(i):
        arrived(from_core.at[i, 1], rc_recv.at[i, 1])
        add_rows(keep.at[i, 1], keep.at[i, 1], from_core.at[i, 1])
        remote(keep.at[i, 1], from_x.at[i], rx_send.at[i], rx_recv.at[i], across)

    def sum_for_along(i):
        arrived(from_core.at[i, 0], rc_recv.at[i, 0])
        arrived(from_x.at[i], rx_recv.at[i])
        add_rows(keep.at[i, 0], keep.at[i, 0], from_core.at[i, 0], from_x.at[i])
        k = steps[i]
        remote(keep.at[i, 0], from_z.at[k], rz_send.at[i], rz_recv.at[k], along(nz - k))

    work(0, 0)
    for i in range(1, nz):
        gathered(i, 0, 0)
        gather_along(i)
        gather_across(i)
        gather_core(i, 0)
        gathered(i - 1, 1, 0)
        gather_core(i - 1, 1)
        work(i - 1, 1)
        work(i, 0)
        if i >= 2:
            sum_for_across(i - 1)
        if i >= 3:
            sum_for_along(i - 2)
    gathered(nz - 1, 1, 0)
    gather_core(nz - 1, 1)
    work(nz - 1, 1)
    if nz >= 3:
        sum_for_along(nz - 2)
    if nz >= 2:
        sum_for_across(nz - 1)
        sum_for_across(0)
        sum_for_along(nz - 1)
    arrived(from_core.at[0, 0], rc_recv.at[0, 0])
    arrived(from_x.at[0], rx_recv.at[0])
    for k in range(1, nz):
        arrived(from_z.at[k], rz_recv.at[k])
    add_rows(out, keep.at[0, 0], from_core.at[0, 0], from_x.at[0], *[from_z.at[k] for k in range(1, nz)])
    for copy, when in sent:
        if when is None:
            copy.wait_send()
        else:
            pl.when(when)(copy.wait_send)


def fused(size, tokens, expert_ids, gate_numer, capacity, up_weight, down_weight):
    nz = size // 4
    block, columns = tokens.shape
    inner = up_weight.shape[2]
    routing = jnp.concatenate([expert_ids, gate_numer], axis=1).astype(jnp.bfloat16).T
    anywhere = pl.BlockSpec(memory_space=pl.ANY)
    near = pl.BlockSpec(memory_space=pltpu.VMEM)
    wide = jnp.bfloat16
    dma = pltpu.SemaphoreType.DMA
    return pl.pallas_call(
        functools.partial(kernel, nz),
        out_shape=jax.ShapeDtypeStruct((block, columns), tokens.dtype),
        in_specs=[anywhere, near, pl.BlockSpec(memory_space=pltpu.SMEM), anywhere, anywhere],
        out_specs=near,
        scratch_shapes=[
            pltpu.VMEM((nz, 2, 2, block, columns), wide),
            pltpu.VMEM((size,) + routing.shape, wide),
            pltpu.VMEM((columns, inner), wide),
            pltpu.VMEM((inner, columns), wide),
            pltpu.VMEM((2 * block, inner), wide),
            pltpu.VMEM((block, block), jnp.float32),
            pltpu.VMEM((nz, 2, block, columns), wide),
            pltpu.VMEM((nz, 2, block, columns), wide),
            pltpu.VMEM((nz, 2, block, columns), wide),
            pltpu.VMEM((nz, block, columns), wide),
            pltpu.VMEM((nz, block, columns), wide),
            dma((3,)), dma((nz + 1,)), dma((nz + 1,)),
            dma((nz + 1,)), dma((nz,)), dma((nz, 2)), dma((nz, 2, 2)),
            dma((nz, 2)), dma((nz, 2)), dma((nz,)), dma((nz,)), dma((nz,)), dma((nz,)),
        ],
        compiler_params=pltpu.CompilerParams(
            collective_id=0, has_side_effects=True, vmem_limit_bytes=56 * 2**20
        ),
        cost_estimate=pl.CostEstimate(
            flops=4 * size * block * columns * inner, bytes_accessed=4 * columns * inner, transcendentals=0
        ),
    )(tokens, routing, capacity, up_weight, down_weight)


def solution(mesh):
    size = mesh.shape["expert"]
    fits = mesh.shape["tensor"] == 1 and size % 4 == 0 and size <= 16
    local = functools.partial(fused, size) if fits else general
    in_specs = (
        P(("group", "expert"), "tensor"),
        P(("group", "expert"), None),
        P(("group", "expert"), None),
        P(),
        P("expert", None, "tensor"),
        P("expert", None, "tensor"),
    )
    out_specs = P(("group", "expert"), "tensor")
    return jax.shard_map(local, mesh=mesh, in_specs=in_specs, out_specs=out_specs, check_vma=False)
```

```python
import functools

import jax
import jax.numpy as jnp
from jax import lax
from jax.experimental import pallas as pl
from jax.experimental.pallas import tpu as pltpu
from jax.sharding import PartitionSpec as P


def entering(part, axis, combine, identity):
    place = lax.axis_index(axis)
    gathered = lax.all_gather(part, axis)
    state = jnp.zeros_like(part) + jnp.asarray(identity, part.dtype)

    def one(lap, state):
        return combine(state, lax.dynamic_index_in_dim(gathered, lap, 0, False))

    return lax.fori_loop(0, place, one, state)


def add_counts(earlier, later):
    return earlier + later


def expert_work(received, up_matrix, down_matrix):
    sources, slot_count, half_width = received.shape
    hidden_half = up_matrix.shape[1]
    fragment = lax.all_gather(received, "tensor", axis=2, tiled=True)
    columns = fragment.shape[2]
    weights_block = up_matrix
    up_total = jnp.dot(
        fragment.reshape(-1, columns), weights_block, preferred_element_type=jnp.float32
    )
    hidden = jax.nn.silu(up_total).astype(jnp.bfloat16).reshape(sources, slot_count, hidden_half)
    fragment = lax.all_gather(hidden, "tensor", axis=2, tiled=True)
    columns = fragment.shape[2]
    weights_block = down_matrix
    down_total = jnp.dot(
        fragment.reshape(-1, columns), weights_block, preferred_element_type=jnp.float32
    )
    return down_total.astype(jnp.bfloat16).reshape(sources, slot_count, half_width)


def general(tokens, expert_ids, gate_numer, capacity, up_weight, down_weight):
    token_rows, half_width = tokens.shape
    per_token = expert_ids.shape[1]
    experts = capacity.shape[0]
    per_source = min(token_rows, 2 * token_rows * per_token // experts)
    chosen = expert_ids.reshape(-1)
    one_hot = (chosen[:, None] == jnp.arange(experts, dtype=jnp.int32)[None, :]).astype(jnp.int32)
    counts = jnp.sum(one_hot, axis=0)
    local_rank = jnp.sum((jnp.cumsum(one_hot, axis=0) - one_hot) * one_hot, axis=1)
    prefix = entering(counts, "expert", add_counts, jnp.zeros_like(counts))
    global_rank = local_rank + jnp.sum(one_hot * prefix[None, :], axis=1)
    limit = jnp.sum(one_hot * capacity[None, :], axis=1)
    retained = global_rank < limit
    numerator = gate_numer.astype(jnp.float32)
    weighting = (numerator / jnp.sum(numerator, axis=1, keepdims=True)).reshape(-1)
    weighting = jnp.where(retained, weighting, jnp.zeros_like(weighting))
    token_of = jnp.arange(token_rows * per_token, dtype=jnp.int32) // per_token
    slot_table = (
        jnp.full((experts, per_source), token_rows, jnp.int32).at[chosen, local_rank].set(token_of)
    )
    source = jnp.concatenate([tokens, jnp.zeros((1, half_width), tokens.dtype)], axis=0)
    up_matrix = up_weight[0]
    down_matrix = down_weight[0]
    outgoing = source[slot_table]
    arrived = lax.all_to_all(outgoing, "expert", split_axis=0, concat_axis=0, tiled=True)
    returned = lax.all_to_all(
        expert_work(arrived, up_matrix, down_matrix),
        "expert",
        split_axis=0,
        concat_axis=0,
        tiled=True,
    )
    picked = returned[chosen, local_rank]
    weighted = picked.astype(jnp.float32) * weighting[:, None]
    mixed = jnp.sum(weighted.reshape(token_rows, per_token, picked.shape[1]), axis=1)
    return mixed.astype(jnp.bfloat16)


def add_rows(dst, *parts):
    @pl.loop(0, dst.shape[0] // 16)
    def _(i):
        rows = pl.ds(pl.multiple_of(i * 16, 16), 16)
        total = parts[0][rows, :].astype(jnp.float32)
        for part in parts[1:]:
            total = total + part[rows, :].astype(jnp.float32)
        dst[rows, :] = total.astype(dst.dtype)


def nearest(at, nz):
    offsets = [0]
    for distance in range(1, nz):
        for source in (at - distance, at + distance):
            if 0 <= source < nz:
                offsets.append((at - source) % nz)
    return offsets


def routed_weights(meta, capacity, weights, place, nz):
    slots, _, block = meta.shape
    half = meta.shape[1] // 2
    c, x, z = place % 2, (place // 2) % 2, place // 4

    def block_of(r):
        cf, xf, k = r // (2 * nz), (r // nz) % 2, r % nz
        zs = z - k
        zs = jnp.where(zs < 0, zs + nz, zs)
        return zs * 4 + (x + xf - 2 * x * xf) * 2 + (c + cf - 2 * c * cf)

    ids = meta[:, :half, :].astype(jnp.float32)
    gates = meta[:, half:, :].astype(jnp.float32)
    hit = (ids == place.astype(jnp.float32)).astype(jnp.float32)
    named = jnp.sum(hit, axis=1)
    gate = jnp.sum(hit * gates, axis=1)
    whole = jnp.sum(gates, axis=1)
    row = lax.broadcasted_iota(jnp.int32, (block, block), 0)
    col = lax.broadcasted_iota(jnp.int32, (block, block), 1)
    earlier = (row < col).astype(jnp.bfloat16)
    inside = jnp.dot(named.astype(jnp.bfloat16), earlier, preferred_element_type=jnp.float32)
    later_slot = lax.broadcasted_iota(jnp.int32, (slots, slots), 0)
    early_slot = lax.broadcasted_iota(jnp.int32, (slots, slots), 1)
    lower = (block_of(early_slot) < block_of(later_slot)).astype(jnp.bfloat16)
    before = jnp.dot(lower, named.astype(jnp.bfloat16), preferred_element_type=jnp.float32)
    rank = inside + jnp.sum(before, axis=1, keepdims=True)
    limit = capacity[place].astype(jnp.float32)
    spread = jnp.where(rank < limit, gate / whole, 0.0)
    weights[...] = jnp.zeros_like(weights)
    weights[0:slots, :] = spread
    weights[...] = weights[...].T


def block_work(rows, hidden, up, down, weights, slot, keep, give):
    width = 256
    block = keep.shape[0]

    @pl.loop(0, up.shape[1] // width)
    def _(i):
        cols = pl.ds(pl.multiple_of(i * width, width), width)
        v = jnp.dot(rows[...].reshape(2 * block, rows.shape[-1]), up[:, cols], preferred_element_type=jnp.float32)
        hidden[:, cols] = (v / (1.0 + jnp.exp(-v))).astype(jnp.bfloat16)

    lane = lax.broadcasted_iota(jnp.int32, weights.shape, 1)
    mine = jnp.sum(jnp.where(lane == slot[0], weights[...], 0.0), axis=1, keepdims=True)
    other = jnp.sum(jnp.where(lane == slot[1], weights[...], 0.0), axis=1, keepdims=True)

    @pl.loop(0, down.shape[1] // width)
    def _(i):
        cols = pl.ds(pl.multiple_of(i * width, width), width)
        v = jnp.dot(hidden[...], down[:, cols], preferred_element_type=jnp.float32)
        keep[:, cols] = (v[:block] * mine).astype(jnp.bfloat16)
        give[:, cols] = (v[block:] * other).astype(jnp.bfloat16)


def kernel(
    nz, tokens_hbm, meta_in, capacity, up_hbm, down_hbm, out,
    held, meta, up, down, hidden, weights, keep, give, from_core, from_x, from_z,
    local_sem, meta_send, meta_recv, gz_send, gx_send, gc_send, g_recv,
    rc_send, rc_recv, rx_send, rx_recv, rz_send, rz_recv,
):
    place = lax.axis_index("expert")
    c, x, z = place % 2, (place // 2) % 2, place // 4
    sibling = place + 1 - 2 * c
    across = place + 2 - 4 * x
    block = tokens_hbm.shape[0]

    def along(k):
        return lax.rem(place + 4 * k, 4 * nz)

    def remote(src, dst, send, recv, target, when=None):
        copy = pltpu.make_async_remote_copy(
            src_ref=src, dst_ref=dst, send_sem=send, recv_sem=recv,
            device_id={"expert": target}, device_id_type=pl.DeviceIdType.MESH,
        )
        if when is None:
            copy.start()
        else:
            pl.when(when)(copy.start)
        sent.append((copy, when))

    def arrived(ref, sem):
        pltpu.make_async_copy(ref, ref, sem).wait()

    sent = []
    parts = 2
    loads = [
        pltpu.make_async_copy(tokens_hbm, held.at[0, 0, 0], local_sem.at[0]),
        pltpu.make_async_copy(up_hbm.at[0], up, local_sem.at[1]),
        pltpu.make_async_copy(down_hbm.at[0], down, local_sem.at[2]),
    ]
    for load in loads:
        load.start()
    meta[0] = meta_in[...]

    barrier = pltpu.get_barrier_semaphore()
    partners = [sibling, across] + [along(k) for k in range(1, nz)]
    for partner in partners:
        pl.semaphore_signal(
            barrier, inc=1, device_id={"expert": partner}, device_id_type=pl.DeviceIdType.MESH
        )
    pl.semaphore_wait(barrier, len(partners))

    steps = [
        functools.reduce(lambda a, s: a + s, [jnp.where(z == at, nearest(at, nz)[i], 0) for at in range(nz)])
        for i in range(nz)
    ]

    def gather_along(i):
        k = steps[i]
        rising = k <= z
        step = jnp.where(rising, 1, -1)
        target = jnp.clip(z + step, 0, nz - 1)
        slot = jnp.clip(k + step, 0, nz - 1)
        remote(
            held.at[k, 0, 0], held.at[slot, 0, 0], gz_send.at[i], g_recv.at[slot, 0, 0],
            place + 4 * (target - z), target != z,
        )

    def gather_own():
        up_z, down_z = jnp.minimum(z + 1, nz - 1), jnp.maximum(z - 1, 0)
        remote(
            held.at[0, 0, 0], held.at[1 % nz, 0, 0], gz_send.at[0], g_recv.at[1 % nz, 0, 0],
            place + 4 * (up_z - z), up_z != z,
        )
        remote(
            held.at[0, 0, 0], held.at[nz - 1, 0, 0], gz_send.at[nz], g_recv.at[nz - 1, 0, 0],
            place + 4 * (down_z - z), down_z != z,
        )

    def gather_across(i):
        k = steps[i]
        remote(held.at[k, 0, 0], held.at[k, 1, 0], gx_send.at[i], g_recv.at[k, 1, 0], across)

    def gather_core(i, xf):
        k = steps[i]
        remote(held.at[k, xf, 0], held.at[k, xf, 1], gc_send.at[i, xf], g_recv.at[k, xf, 1], sibling)

    def gathered(i, xf, cf):
        k = steps[i]
        arrived(held.at[k, xf, cf], g_recv.at[k, xf, cf])

    for k in range(1, nz):
        remote(meta.at[0], meta.at[k], meta_send.at[k], meta_recv.at[k], along(k))
    loads[0].wait()
    gather_own()
    gather_core(0, 0)
    for k in range(1, nz):
        arrived(meta.at[k], meta_recv.at[k])
    remote(meta.at[0:nz], meta.at[nz : 2 * nz], meta_send.at[0], meta_recv.at[0], across)
    gather_across(0)
    arrived(meta.at[nz : 2 * nz], meta_recv.at[0])
    remote(meta.at[0 : 2 * nz], meta.at[2 * nz : 4 * nz], meta_send.at[nz], meta_recv.at[nz], sibling)
    arrived(meta.at[2 * nz : 4 * nz], meta_recv.at[nz])
    routed_weights(meta, capacity, weights, place, nz)
    loads[1].wait()
    loads[2].wait()

    def work(i, xf):
        gathered(i, xf, 1)
        k = steps[i]
        slot = (xf * nz + k, (2 + xf) * nz + k)
        block_work(held.at[k, xf], hidden, up, down, weights, slot, keep.at[i, xf], give.at[i, xf])
        remote(give.at[i, xf], from_core.at[i, xf], rc_send.at[i, xf], rc_recv.at[i, xf], sibling)

    pieces = [pl.ds(at * (block // parts), block // parts) for at in range(parts)]

    def sum_for_across(i):
        arrived(from_core.at[i, 1], rc_recv.at[i, 1])
        for p, rows in enumerate(pieces):
            mine = keep.at[i, 1, rows]
            add_rows(mine, mine, from_core.at[i, 1, rows])
            remote(mine, from_x.at[i, rows], rx_send.at[i, p], rx_recv.at[i, p], across)

    def sum_for_along(i):
        arrived(from_core.at[i, 0], rc_recv.at[i, 0])
        k = steps[i]
        for p, rows in enumerate(pieces):
            mine = keep.at[i, 0, rows]
            arrived(from_x.at[i, rows], rx_recv.at[i, p])
            add_rows(mine, mine, from_core.at[i, 0, rows], from_x.at[i, rows])
            remote(mine, from_z.at[k, rows], rz_send.at[i, p], rz_recv.at[k, p], along(nz - k))

    work(0, 0)
    for i in range(1, nz):
        gathered(i, 0, 0)
        gather_along(i)
        gather_across(i)
        gather_core(i, 0)
        gathered(i - 1, 1, 0)
        gather_core(i - 1, 1)
        work(i - 1, 1)
        work(i, 0)
        if i >= 2:
            sum_for_across(i - 1)
        if i >= 3:
            sum_for_along(i - 2)
    gathered(nz - 1, 1, 0)
    gather_core(nz - 1, 1)
    work(nz - 1, 1)
    if nz >= 3:
        sum_for_along(nz - 2)
    if nz >= 2:
        sum_for_across(nz - 1)
        sum_for_across(0)
        sum_for_along(nz - 1)
    arrived(from_core.at[0, 0], rc_recv.at[0, 0])
    for p, rows in enumerate(pieces):
        arrived(from_x.at[0, rows], rx_recv.at[0, p])
        for k in range(1, nz):
            arrived(from_z.at[k, rows], rz_recv.at[k, p])
        others = [from_z.at[k, rows] for k in range(1, nz)]
        add_rows(out.at[rows], keep.at[0, 0, rows], from_core.at[0, 0, rows], from_x.at[0, rows], *others)
    for copy, when in sent:
        if when is None:
            copy.wait_send()
        else:
            pl.when(when)(copy.wait_send)


def fused(size, tokens, expert_ids, gate_numer, capacity, up_weight, down_weight):
    nz = size // 4
    block, columns = tokens.shape
    inner = up_weight.shape[2]
    routing = jnp.concatenate([expert_ids, gate_numer], axis=1).astype(jnp.bfloat16).T
    anywhere = pl.BlockSpec(memory_space=pl.ANY)
    near = pl.BlockSpec(memory_space=pltpu.VMEM)
    wide = jnp.bfloat16
    dma = pltpu.SemaphoreType.DMA
    return pl.pallas_call(
        functools.partial(kernel, nz),
        out_shape=jax.ShapeDtypeStruct((block, columns), tokens.dtype),
        in_specs=[anywhere, near, pl.BlockSpec(memory_space=pltpu.SMEM), anywhere, anywhere],
        out_specs=near,
        scratch_shapes=[
            pltpu.VMEM((nz, 2, 2, block, columns), wide),
            pltpu.VMEM((size,) + routing.shape, wide),
            pltpu.VMEM((columns, inner), wide),
            pltpu.VMEM((inner, columns), wide),
            pltpu.VMEM((2 * block, inner), wide),
            pltpu.VMEM((block, block), jnp.float32),
            pltpu.VMEM((nz, 2, block, columns), wide),
            pltpu.VMEM((nz, 2, block, columns), wide),
            pltpu.VMEM((nz, 2, block, columns), wide),
            pltpu.VMEM((nz, block, columns), wide),
            pltpu.VMEM((nz, block, columns), wide),
            dma((3,)), dma((nz + 1,)), dma((nz + 1,)),
            dma((nz + 1,)), dma((nz,)), dma((nz, 2)), dma((nz, 2, 2)),
            dma((nz, 2)), dma((nz, 2)), dma((nz, 2)), dma((nz, 2)), dma((nz, 2)), dma((nz, 2)),
        ],
        compiler_params=pltpu.CompilerParams(
            collective_id=0, has_side_effects=True, vmem_limit_bytes=56 * 2**20
        ),
        cost_estimate=pl.CostEstimate(
            flops=4 * size * block * columns * inner, bytes_accessed=4 * columns * inner, transcendentals=0
        ),
    )(tokens, routing, capacity, up_weight, down_weight)


def solution(mesh):
    size = mesh.shape["expert"]
    fits = mesh.shape["tensor"] == 1 and size % 4 == 0 and size <= 16
    local = functools.partial(fused, size) if fits else general
    in_specs = (
        P(("group", "expert"), "tensor"),
        P(("group", "expert"), None),
        P(("group", "expert"), None),
        P(),
        P("expert", None, "tensor"),
        P("expert", None, "tensor"),
    )
    out_specs = P(("group", "expert"), "tensor")
    return jax.shard_map(local, mesh=mesh, in_specs=in_specs, out_specs=out_specs, check_vma=False)
```

```python
import functools

import jax
import jax.numpy as jnp
from jax import lax
from jax.experimental import pallas as pl
from jax.experimental.pallas import tpu as pltpu
from jax.sharding import PartitionSpec as P


def entering(part, axis, combine, identity):
    place = lax.axis_index(axis)
    gathered = lax.all_gather(part, axis)
    state = jnp.zeros_like(part) + jnp.asarray(identity, part.dtype)

    def one(lap, state):
        return combine(state, lax.dynamic_index_in_dim(gathered, lap, 0, False))

    return lax.fori_loop(0, place, one, state)


def add_counts(earlier, later):
    return earlier + later


def expert_work(received, up_matrix, down_matrix):
    sources, slot_count, half_width = received.shape
    hidden_half = up_matrix.shape[1]
    fragment = lax.all_gather(received, "tensor", axis=2, tiled=True)
    columns = fragment.shape[2]
    weights_block = up_matrix
    up_total = jnp.dot(
        fragment.reshape(-1, columns), weights_block, preferred_element_type=jnp.float32
    )
    hidden = jax.nn.silu(up_total).astype(jnp.bfloat16).reshape(sources, slot_count, hidden_half)
    fragment = lax.all_gather(hidden, "tensor", axis=2, tiled=True)
    columns = fragment.shape[2]
    weights_block = down_matrix
    down_total = jnp.dot(
        fragment.reshape(-1, columns), weights_block, preferred_element_type=jnp.float32
    )
    return down_total.astype(jnp.bfloat16).reshape(sources, slot_count, half_width)


def general(tokens, expert_ids, gate_numer, capacity, up_weight, down_weight):
    token_rows, half_width = tokens.shape
    per_token = expert_ids.shape[1]
    experts = capacity.shape[0]
    per_source = min(token_rows, 2 * token_rows * per_token // experts)
    chosen = expert_ids.reshape(-1)
    one_hot = (chosen[:, None] == jnp.arange(experts, dtype=jnp.int32)[None, :]).astype(jnp.int32)
    counts = jnp.sum(one_hot, axis=0)
    local_rank = jnp.sum((jnp.cumsum(one_hot, axis=0) - one_hot) * one_hot, axis=1)
    prefix = entering(counts, "expert", add_counts, jnp.zeros_like(counts))
    global_rank = local_rank + jnp.sum(one_hot * prefix[None, :], axis=1)
    limit = jnp.sum(one_hot * capacity[None, :], axis=1)
    retained = global_rank < limit
    numerator = gate_numer.astype(jnp.float32)
    weighting = (numerator / jnp.sum(numerator, axis=1, keepdims=True)).reshape(-1)
    weighting = jnp.where(retained, weighting, jnp.zeros_like(weighting))
    token_of = jnp.arange(token_rows * per_token, dtype=jnp.int32) // per_token
    slot_table = (
        jnp.full((experts, per_source), token_rows, jnp.int32).at[chosen, local_rank].set(token_of)
    )
    source = jnp.concatenate([tokens, jnp.zeros((1, half_width), tokens.dtype)], axis=0)
    up_matrix = up_weight[0]
    down_matrix = down_weight[0]
    outgoing = source[slot_table]
    arrived = lax.all_to_all(outgoing, "expert", split_axis=0, concat_axis=0, tiled=True)
    returned = lax.all_to_all(
        expert_work(arrived, up_matrix, down_matrix),
        "expert",
        split_axis=0,
        concat_axis=0,
        tiled=True,
    )
    picked = returned[chosen, local_rank]
    weighted = picked.astype(jnp.float32) * weighting[:, None]
    mixed = jnp.sum(weighted.reshape(token_rows, per_token, picked.shape[1]), axis=1)
    return mixed.astype(jnp.bfloat16)


def add_rows(dst, *parts):
    @pl.loop(0, dst.shape[0] // 16)
    def _(i):
        rows = pl.ds(pl.multiple_of(i * 16, 16), 16)
        total = parts[0][rows, :].astype(jnp.float32)
        for part in parts[1:]:
            total = total + part[rows, :].astype(jnp.float32)
        dst[rows, :] = total.astype(dst.dtype)


def nearest(at, nz):
    offsets = [0]
    for distance in range(1, nz):
        for source in (at - distance, at + distance):
            if 0 <= source < nz:
                offsets.append((at - source) % nz)
    return offsets


def routed_weights(meta, capacity, weights, place, nz):
    slots, _, block = meta.shape
    half = meta.shape[1] // 2
    c, x, z = place % 2, (place // 2) % 2, place // 4

    def block_of(r):
        cf, xf, k = r // (2 * nz), (r // nz) % 2, r % nz
        zs = z - k
        zs = jnp.where(zs < 0, zs + nz, zs)
        return zs * 4 + (x + xf - 2 * x * xf) * 2 + (c + cf - 2 * c * cf)

    ids = meta[:, :half, :].astype(jnp.float32)
    gates = meta[:, half:, :].astype(jnp.float32)
    hit = (ids == place.astype(jnp.float32)).astype(jnp.float32)
    named = jnp.sum(hit, axis=1)
    gate = jnp.sum(hit * gates, axis=1)
    whole = jnp.sum(gates, axis=1)
    row = lax.broadcasted_iota(jnp.int32, (block, block), 0)
    col = lax.broadcasted_iota(jnp.int32, (block, block), 1)
    earlier = (row < col).astype(jnp.bfloat16)
    inside = jnp.dot(named.astype(jnp.bfloat16), earlier, preferred_element_type=jnp.float32)
    later_slot = lax.broadcasted_iota(jnp.int32, (slots, slots), 0)
    early_slot = lax.broadcasted_iota(jnp.int32, (slots, slots), 1)
    lower = (block_of(early_slot) < block_of(later_slot)).astype(jnp.bfloat16)
    before = jnp.dot(lower, named.astype(jnp.bfloat16), preferred_element_type=jnp.float32)
    rank = inside + jnp.sum(before, axis=1, keepdims=True)
    limit = capacity[place].astype(jnp.float32)
    spread = jnp.where(rank < limit, gate / whole, 0.0)
    weights[...] = jnp.zeros_like(weights)
    weights[0:slots, :] = spread
    weights[...] = weights[...].T


def block_work(rows, hidden, up, down, weights, slot, keep, give):
    width = 256
    block = keep.shape[0]

    @pl.loop(0, up.shape[1] // width)
    def _(i):
        cols = pl.ds(pl.multiple_of(i * width, width), width)
        v = jnp.dot(rows[...].reshape(2 * block, rows.shape[-1]), up[:, cols], preferred_element_type=jnp.float32)
        hidden[:, cols] = (v / (1.0 + jnp.exp(-v))).astype(jnp.bfloat16)

    lane = lax.broadcasted_iota(jnp.int32, weights.shape, 1)
    mine = jnp.sum(jnp.where(lane == slot[0], weights[...], 0.0), axis=1, keepdims=True)
    other = jnp.sum(jnp.where(lane == slot[1], weights[...], 0.0), axis=1, keepdims=True)

    @pl.loop(0, down.shape[1] // width)
    def _(i):
        cols = pl.ds(pl.multiple_of(i * width, width), width)
        v = jnp.dot(hidden[...], down[:, cols], preferred_element_type=jnp.float32)
        keep[:, cols] = (v[:block] * mine).astype(jnp.bfloat16)
        give[:, cols] = (v[block:] * other).astype(jnp.bfloat16)


def kernel(
    nz, tokens_hbm, meta_in, capacity, up_hbm, down_hbm, out,
    held, meta, up, down, hidden, weights, keep, give, from_core, from_x, from_z,
    local_sem, meta_send, meta_recv, gz_send, gx_send, gc_send, g_recv,
    rc_send, rc_recv, rx_send, rx_recv, rz_send, rz_recv,
):
    place = lax.axis_index("expert")
    c, x, z = place % 2, (place // 2) % 2, place // 4
    sibling = place + 1 - 2 * c
    across = place + 2 - 4 * x
    block = tokens_hbm.shape[0]

    def along(k):
        return lax.rem(place + 4 * k, 4 * nz)

    def remote(src, dst, send, recv, target, when=None):
        copy = pltpu.make_async_remote_copy(
            src_ref=src, dst_ref=dst, send_sem=send, recv_sem=recv,
            device_id={"expert": target}, device_id_type=pl.DeviceIdType.MESH,
        )
        if when is None:
            copy.start()
        else:
            pl.when(when)(copy.start)
        sent.append((copy, when))

    def arrived(ref, sem):
        pltpu.make_async_copy(ref, ref, sem).wait()

    sent = []
    parts = 4
    loads = [
        pltpu.make_async_copy(tokens_hbm, held.at[0, 0, 0], local_sem.at[0]),
        pltpu.make_async_copy(up_hbm.at[0], up, local_sem.at[1]),
        pltpu.make_async_copy(down_hbm.at[0], down, local_sem.at[2]),
    ]
    for load in loads:
        load.start()
    meta[0] = meta_in[...]

    barrier = pltpu.get_barrier_semaphore()
    partners = [sibling, across] + [along(k) for k in range(1, nz)]
    for partner in partners:
        pl.semaphore_signal(
            barrier, inc=1, device_id={"expert": partner}, device_id_type=pl.DeviceIdType.MESH
        )
    pl.semaphore_wait(barrier, len(partners))

    steps = [
        functools.reduce(lambda a, s: a + s, [jnp.where(z == at, nearest(at, nz)[i], 0) for at in range(nz)])
        for i in range(nz)
    ]

    def gather_along(i):
        k = steps[i]
        rising = k <= z
        step = jnp.where(rising, 1, -1)
        target = jnp.clip(z + step, 0, nz - 1)
        slot = jnp.clip(k + step, 0, nz - 1)
        remote(
            held.at[k, 0, 0], held.at[slot, 0, 0], gz_send.at[i], g_recv.at[slot, 0, 0],
            place + 4 * (target - z), target != z,
        )

    def gather_own():
        up_z, down_z = jnp.minimum(z + 1, nz - 1), jnp.maximum(z - 1, 0)
        remote(
            held.at[0, 0, 0], held.at[1 % nz, 0, 0], gz_send.at[0], g_recv.at[1 % nz, 0, 0],
            place + 4 * (up_z - z), up_z != z,
        )
        remote(
            held.at[0, 0, 0], held.at[nz - 1, 0, 0], gz_send.at[nz], g_recv.at[nz - 1, 0, 0],
            place + 4 * (down_z - z), down_z != z,
        )

    def gather_across(i):
        k = steps[i]
        remote(held.at[k, 0, 0], held.at[k, 1, 0], gx_send.at[i], g_recv.at[k, 1, 0], across)

    def gather_core(i, xf):
        k = steps[i]
        remote(held.at[k, xf, 0], held.at[k, xf, 1], gc_send.at[i, xf], g_recv.at[k, xf, 1], sibling)

    def gathered(i, xf, cf):
        k = steps[i]
        arrived(held.at[k, xf, cf], g_recv.at[k, xf, cf])

    for k in range(1, nz):
        remote(meta.at[0], meta.at[k], meta_send.at[k], meta_recv.at[k], along(k))
    loads[0].wait()
    gather_own()
    gather_core(0, 0)
    for k in range(1, nz):
        arrived(meta.at[k], meta_recv.at[k])
    remote(meta.at[0:nz], meta.at[nz : 2 * nz], meta_send.at[0], meta_recv.at[0], across)
    gather_across(0)
    arrived(meta.at[nz : 2 * nz], meta_recv.at[0])
    remote(meta.at[0 : 2 * nz], meta.at[2 * nz : 4 * nz], meta_send.at[nz], meta_recv.at[nz], sibling)
    arrived(meta.at[2 * nz : 4 * nz], meta_recv.at[nz])
    routed_weights(meta, capacity, weights, place, nz)
    loads[1].wait()
    loads[2].wait()

    def work(i, xf):
        gathered(i, xf, 1)
        k = steps[i]
        slot = (xf * nz + k, (2 + xf) * nz + k)
        block_work(held.at[k, xf], hidden, up, down, weights, slot, keep.at[i, xf], give.at[i, xf])
        remote(give.at[i, xf], from_core.at[i, xf], rc_send.at[i, xf], rc_recv.at[i, xf], sibling)

    pieces = [pl.ds(at * (block // parts), block // parts) for at in range(parts)]

    def sum_for_across(i):
        arrived(from_core.at[i, 1], rc_recv.at[i, 1])
        for p, rows in enumerate(pieces):
            mine = keep.at[i, 1, rows]
            add_rows(mine, mine, from_core.at[i, 1, rows])
            remote(mine, from_x.at[i, rows], rx_send.at[i, p], rx_recv.at[i, p], across)

    def sum_for_along(i):
        arrived(from_core.at[i, 0], rc_recv.at[i, 0])
        k = steps[i]
        for p, rows in enumerate(pieces):
            mine = keep.at[i, 0, rows]
            arrived(from_x.at[i, rows], rx_recv.at[i, p])
            add_rows(mine, mine, from_core.at[i, 0, rows], from_x.at[i, rows])
            remote(mine, from_z.at[k, rows], rz_send.at[i, p], rz_recv.at[k, p], along(nz - k))

    work(0, 0)
    for i in range(1, nz):
        gathered(i, 0, 0)
        gather_along(i)
        gather_across(i)
        gather_core(i, 0)
        gathered(i - 1, 1, 0)
        gather_core(i - 1, 1)
        work(i - 1, 1)
        work(i, 0)
        if i >= 2:
            sum_for_across(i - 1)
        if i >= 3:
            sum_for_along(i - 2)
    gathered(nz - 1, 1, 0)
    gather_core(nz - 1, 1)
    work(nz - 1, 1)
    if nz >= 3:
        sum_for_along(nz - 2)
    if nz >= 2:
        sum_for_across(nz - 1)
        sum_for_across(0)
        sum_for_along(nz - 1)
    arrived(from_core.at[0, 0], rc_recv.at[0, 0])
    for p, rows in enumerate(pieces):
        arrived(from_x.at[0, rows], rx_recv.at[0, p])
        for k in range(1, nz):
            arrived(from_z.at[k, rows], rz_recv.at[k, p])
        others = [from_z.at[k, rows] for k in range(1, nz)]
        add_rows(out.at[rows], keep.at[0, 0, rows], from_core.at[0, 0, rows], from_x.at[0, rows], *others)
    for copy, when in sent:
        if when is None:
            copy.wait_send()
        else:
            pl.when(when)(copy.wait_send)


def fused(size, tokens, expert_ids, gate_numer, capacity, up_weight, down_weight):
    nz = size // 4
    block, columns = tokens.shape
    inner = up_weight.shape[2]
    routing = jnp.concatenate([expert_ids, gate_numer], axis=1).astype(jnp.bfloat16).T
    anywhere = pl.BlockSpec(memory_space=pl.ANY)
    near = pl.BlockSpec(memory_space=pltpu.VMEM)
    wide = jnp.bfloat16
    dma = pltpu.SemaphoreType.DMA
    return pl.pallas_call(
        functools.partial(kernel, nz),
        out_shape=jax.ShapeDtypeStruct((block, columns), tokens.dtype),
        in_specs=[anywhere, near, pl.BlockSpec(memory_space=pltpu.SMEM), anywhere, anywhere],
        out_specs=near,
        scratch_shapes=[
            pltpu.VMEM((nz, 2, 2, block, columns), wide),
            pltpu.VMEM((size,) + routing.shape, wide),
            pltpu.VMEM((columns, inner), wide),
            pltpu.VMEM((inner, columns), wide),
            pltpu.VMEM((2 * block, inner), wide),
            pltpu.VMEM((block, block), jnp.float32),
            pltpu.VMEM((nz, 2, block, columns), wide),
            pltpu.VMEM((nz, 2, block, columns), wide),
            pltpu.VMEM((nz, 2, block, columns), wide),
            pltpu.VMEM((nz, block, columns), wide),
            pltpu.VMEM((nz, block, columns), wide),
            dma((3,)), dma((nz + 1,)), dma((nz + 1,)),
            dma((nz + 1,)), dma((nz,)), dma((nz, 2)), dma((nz, 2, 2)),
            dma((nz, 2)), dma((nz, 2)), dma((nz, 4)), dma((nz, 4)), dma((nz, 4)), dma((nz, 4)),
        ],
        compiler_params=pltpu.CompilerParams(
            collective_id=0, has_side_effects=True, vmem_limit_bytes=56 * 2**20
        ),
        cost_estimate=pl.CostEstimate(
            flops=4 * size * block * columns * inner, bytes_accessed=4 * columns * inner, transcendentals=0
        ),
    )(tokens, routing, capacity, up_weight, down_weight)


def solution(mesh):
    size = mesh.shape["expert"]
    fits = mesh.shape["tensor"] == 1 and size % 4 == 0 and size <= 16
    local = functools.partial(fused, size) if fits else general
    in_specs = (
        P(("group", "expert"), "tensor"),
        P(("group", "expert"), None),
        P(("group", "expert"), None),
        P(),
        P("expert", None, "tensor"),
        P("expert", None, "tensor"),
    )
    out_specs = P(("group", "expert"), "tensor")
    return jax.shard_map(local, mesh=mesh, in_specs=in_specs, out_specs=out_specs, check_vma=False)
```
